32 devices in a mesh: groups: 2 (over y), expert: 4 (over z), dp: 2 (over x), sub: 2 (over core).
Axes of the slice: x: 2, y: 2, z: 4, core: 2. Of those that a mesh axis runs over, the one named last changes fastest.
Arguments:
- tokens: bfloat16 [4096, 2048], P(('groups', 'expert', 'dp', 'sub')), parts along dimension 0, may hold values from -6 to 6
- cotangent: bfloat16 [4096, 2048], P(('groups', 'expert', 'dp', 'sub')), parts along dimension 0, may hold values from -6 to 6
- gate_prob: float32 [4096], P(('groups', 'expert', 'dp', 'sub')), parts along dimension 0, may hold values from 0.25 to 1
- target_device: int32 [4096], P(('groups', 'expert', 'dp', 'sub')), parts along dimension 0, may hold values from 0 to 3, as said below
- use_copy: int32 [4096], P(('groups', 'expert', 'dp', 'sub')), parts along dimension 0, may hold values from 0 to 1
- hot_experts: int32 [4], P('groups'), parts along dimension 0, may hold values from 0 to 3, as said below
- copy_slot: int32 [8], P('groups'), parts along dimension 0, may hold values from 0 to 1, as said below
- gate_weight: bfloat16 [4, 2048, 768], P('expert', None, 'sub'), may hold values from -0.125 to 0.125
- up_weight: bfloat16 [4, 2048, 768], P('expert', None, 'sub'), may hold values from -0.125 to 0.125
- down_weight: bfloat16 [4, 768, 2048], P('expert', 'sub'), may hold values from -0.21875 to 0.21875
Outputs:
- layer_out: bfloat16 [4096, 2048], P(('groups', 'expert', 'dp', 'sub')), parts along dimension 0
- token_grad: bfloat16 [4096, 2048], P(('groups', 'expert', 'dp', 'sub')), parts along dimension 0
- prob_grad: float32 [4096], P(('groups', 'expert', 'dp', 'sub')), parts along dimension 0
- gate_weight_grad: float32 [8, 2048, 768], P(('groups', 'expert'), 'dp', 'sub'), parts along dimension 0
- up_weight_grad: float32 [8, 2048, 768], P(('groups', 'expert'), 'dp', 'sub'), parts along dimension 0
- down_weight_grad: float32 [8, 768, 2048], P(('groups', 'expert'), 'sub', 'dp'), parts along dimension 0
The draws below stay inside these ranges and needn't reach their ends.
There are 2 independent parts, one for each index of `groups`. The reference program is written for one: setup_inputs(seed, part) draws one part's arguments, and reference() takes and returns one part's arrays. A program takes and returns all parts, laid end to end along the dimension named above; an argument that names none is the same for every part. Nothing has to cross between parts.
Inputs may be any that keep to these rules, and one draw needn't show every extreme that they name: Among the 128 rows of one device, at most 24 have any one pair of target_device and use_copy; in every such block some pair has exactly 24 rows, and the pair (hot_experts[0], 0) has exactly 24 rows in every block. `hot_experts`: distinct experts. copy_slot[hot_experts[0]] = 1 and copy_slot[hot_experts[1]] = 0: a hot expert's own device holds the other one's copy.
All inputs are finite; a program needn't handle non-finite values.
Results may differ from the reference program's by a relative error of at most 0.0095.
Values may be sent and summed in bfloat16 or wider, within the bound.
A program may use at most 128 MiB of HBM per device.

```python
import jax
import jax.numpy as jnp
from jax import lax

D = 2048
FF = 768
TOK_DEV = 128
NHOT = 2
EXPERTS = 4
CAP = 24
TOKENS = 2048
N_EXPERT = 4
N_DP = 2
N_SUB = 2


def hot_plan(key):
    base = jax.random.fold_in(key, 101)
    order = jax.random.permutation(base, N_EXPERT)
    chosen_hot = order[:NHOT].astype(jnp.int32)
    slots = jax.random.randint(jax.random.fold_in(key, 102), (N_EXPERT,), 0, NHOT, dtype=jnp.int32)
    slots = slots.at[chosen_hot[0]].set(1).at[chosen_hot[1]].set(0)
    return (chosen_hot, slots)


def route_plan(key):
    chosen_hot, slots = hot_plan(key)
    devices = N_EXPERT * N_DP * N_SUB
    slot_total = 2 * N_EXPERT * CAP
    slot_class = jnp.arange(slot_total, dtype=jnp.int32) // CAP
    scores = jax.random.randint(jax.random.fold_in(key, 103), (devices, slot_total), 0, 65536, dtype=jnp.int32)
    extra_class = jax.random.randint(jax.random.fold_in(key, 104), (devices, 1), 0, 2 * N_EXPERT, dtype=jnp.int32)
    forced = (slot_class[None, :] == 2 * chosen_hot[0]) | (slot_class[None, :] == extra_class)
    favored = slot_class[None, :] == 2 * chosen_hot[1]
    scores = scores + jnp.where(forced, 131072, 0) + jnp.where(favored, 32768, 0)
    keyed = scores * slot_total + jnp.arange(slot_total, dtype=jnp.int32)[None, :]
    unused, chosen = lax.top_k(keyed, TOK_DEV)
    shuffle = jax.random.randint(jax.random.fold_in(key, 105), (devices, TOK_DEV), 0, 65536, dtype=jnp.int32)
    shuffle = shuffle * TOK_DEV + jnp.arange(TOK_DEV, dtype=jnp.int32)[None, :]
    order = jnp.argsort(shuffle, axis=1, stable=True)
    chosen = jnp.take_along_axis(chosen, order, axis=1)
    class_of = (chosen // CAP).reshape(-1).astype(jnp.int32)
    return (class_of // 2, class_of % 2)


def draw_target_device(key, part):
    return route_plan(key)[0]


def draw_use_copy(key, part):
    return route_plan(key)[1]


def draw_hot_experts(key, part):
    return hot_plan(key)[0]


def draw_copy_slot(key, part):
    return hot_plan(key)[1]


def steps_of(rng, shape, split, least, top_value):
    gain, own = 1.0, jax.random.fold_in(rng, 6)
    for position, shards_of in split:
        heights = jnp.exp(jax.random.uniform(jax.random.fold_in(own, position), (shards_of,), jnp.float32, least / len(split), top_value / len(split)))
        gain = gain * jnp.repeat(heights, shape[position] // shards_of).reshape([-1 if axis == position else 1 for axis in range(len(shape))])
    return gain


def normal_values(key, shape, spread, most, shards=(), held_as=jnp.bfloat16):
    array = jax.random.normal(key, shape, jnp.float32) * spread
    if len(shards) > 0:
        array = steps_of(key, shape, shards, -0.22, 0.18) * array
    return jnp.clip(array, min=-most, max=most).astype(held_as)


def setup_inputs(seed: int = 0, part: int = 0) -> dict:
    key_list = jax.random.split(jax.random.key(seed), 11)
    part_splits = jax.random.split(jax.random.fold_in(key_list[10], part), 11)
    tokens = normal_values(part_splits[0], (TOKENS, D), 1.0, 6.0, ((0, 16),))
    cotangent = normal_values(part_splits[1], (TOKENS, D), 1.0, 6.0, ((0, 16),))
    gate_prob = jnp.clip(0.25 + 0.75 * jax.random.uniform(part_splits[2], (TOKENS,), jnp.float32) ** steps_of(part_splits[2], (TOKENS,), ((0, 16),), -0.2, 0.2), 0.25, 1.0)
    target_device = draw_target_device(jax.random.fold_in(jax.random.fold_in(key_list[10], part), 71), part)
    use_copy = draw_use_copy(jax.random.fold_in(jax.random.fold_in(key_list[10], part), 71), part)
    hot_experts = draw_hot_experts(jax.random.fold_in(jax.random.fold_in(key_list[10], part), 71), part)
    copy_slot = draw_copy_slot(jax.random.fold_in(jax.random.fold_in(key_list[10], part), 71), part)
    gate_weight = normal_values(key_list[7], (EXPERTS, D, FF), D ** -0.5, 0.125, ((0, 4), (2, 2)))
    up_weight = normal_values(key_list[8], (EXPERTS, D, FF), D ** -0.5, 0.125, ((0, 4), (2, 2)))
    down_weight = normal_values(key_list[9], (EXPERTS, FF, D), FF ** -0.5, 0.21875, ((0, 4), (1, 2)))
    return {"tokens": tokens, "cotangent": cotangent, "gate_prob": gate_prob, "target_device": target_device, "use_copy": use_copy, "hot_experts": hot_experts, "copy_slot": copy_slot, "gate_weight": gate_weight, "up_weight": up_weight, "down_weight": down_weight}


def expert_pass(rows_in, scaled_rows, gate_weight, up_weight, down_weight):
    gate_in = jnp.dot(rows_in, gate_weight, preferred_element_type=jnp.float32)
    up_in = jnp.dot(rows_in, up_weight, preferred_element_type=jnp.float32)
    sigmoid_gate = jax.nn.sigmoid(gate_in)
    active = gate_in * sigmoid_gate
    hidden = (active * up_in).astype(jnp.bfloat16)
    out_rows = jnp.dot(hidden, down_weight, preferred_element_type=jnp.float32).astype(jnp.bfloat16)
    hidden_grad = jnp.dot(scaled_rows, down_weight.T, preferred_element_type=jnp.float32)
    gate_grad = (hidden_grad * up_in * sigmoid_gate * (1.0 + gate_in * (1.0 - sigmoid_gate))).astype(jnp.bfloat16)
    up_grad = (hidden_grad * active).astype(jnp.bfloat16)
    row_grad = jnp.dot(gate_grad, gate_weight.T, preferred_element_type=jnp.float32)
    row_grad = (row_grad + jnp.dot(up_grad, up_weight.T, preferred_element_type=jnp.float32)).astype(jnp.bfloat16)
    return out_rows, row_grad, hidden, gate_grad, up_grad


def summed_parts(left, right):
    product = jnp.einsum("grk,grf->gkf", left.astype(jnp.float32), right.astype(jnp.float32), precision=lax.Precision.HIGHEST)
    rounded = lax.optimization_barrier(product.astype(jnp.bfloat16))
    return jnp.sum(rounded.astype(jnp.float32), axis=0)


def reference(tokens, cotangent, gate_prob, target_device, use_copy, hot_experts, copy_slot, gate_weight, up_weight, down_weight):
    row_block = jnp.arange(TOKENS, dtype=jnp.int32) // TOK_DEV
    src_expert = row_block // (N_DP * N_SUB)
    src_dp = (row_block // N_SUB) % N_DP
    src_sub = row_block % N_SUB
    slot_class = target_device * 2 + use_copy
    member = (slot_class[:, None] == jnp.arange(2 * EXPERTS, dtype=jnp.int32)[None, :]).astype(jnp.int32)
    member = member.reshape(TOKENS // TOK_DEV, TOK_DEV, 2 * EXPERTS)
    earlier = jnp.cumsum(member, axis=1) - member
    slot_rank = jnp.sum(earlier * member, axis=2).reshape(TOKENS)
    group_rows = EXPERTS * N_SUB * CAP
    buffer_index = ((((target_device * N_DP + src_dp) * 2 + use_copy) * EXPERTS + src_expert) * N_SUB + src_sub) * CAP + slot_rank
    buffer_index = buffer_index.astype(jnp.int32)
    total_rows = EXPERTS * N_DP * 2 * group_rows
    scaled = (gate_prob[:, None] * cotangent.astype(jnp.float32)).astype(jnp.bfloat16)
    rows_buffer = jnp.zeros((total_rows, D), tokens.dtype).at[buffer_index].set(tokens)
    rows_buffer = rows_buffer.reshape(EXPERTS, N_DP, 2, group_rows, D)
    scaled_buffer = jnp.zeros((total_rows, D), scaled.dtype).at[buffer_index].set(scaled)
    scaled_buffer = scaled_buffer.reshape(EXPERTS, N_DP, 2, group_rows, D)
    copy_expert = hot_experts[copy_slot].astype(jnp.int32)

    def per_device(packed):
        rows_here, scaled_here, home, copied = packed
        results = []
        for kind, expert in ((0, home), (1, copied)):
            rows_in = rows_here[:, kind].reshape(N_DP * group_rows, D)
            scaled_rows = scaled_here[:, kind].reshape(N_DP * group_rows, D)
            out_rows, row_grad, hidden, gate_grad, up_grad = expert_pass(rows_in, scaled_rows, gate_weight[expert], up_weight[expert], down_weight[expert])
            rows_grouped = rows_in.reshape(N_DP, group_rows, D)
            scaled_grouped = scaled_rows.reshape(N_DP, group_rows, D)
            parts = (summed_parts(rows_grouped, gate_grad.reshape(N_DP, group_rows, FF)),
                     summed_parts(rows_grouped, up_grad.reshape(N_DP, group_rows, FF)),
                     summed_parts(hidden.reshape(N_DP, group_rows, FF), scaled_grouped))
            results.append((out_rows.reshape(N_DP, group_rows, D), row_grad.reshape(N_DP, group_rows, D), parts))
        outputs = jnp.stack((results[0][0], results[1][0]), axis=1)
        row_grads = jnp.stack((results[0][1], results[1][1]), axis=1)
        own_parts = results[0][2]
        copy_parts = (results[1][2][0].astype(jnp.bfloat16), results[1][2][1].astype(jnp.bfloat16), results[1][2][2].astype(jnp.bfloat16))
        return outputs, row_grads, own_parts, copy_parts

    homes = jnp.arange(EXPERTS, dtype=jnp.int32)
    outputs, row_grads, own_parts, copy_parts = lax.map(per_device, (rows_buffer, scaled_buffer, homes, copy_expert))
    out_flat = outputs.reshape(total_rows, D)[buffer_index]
    grad_flat = row_grads.reshape(total_rows, D)[buffer_index]
    layer_out = (gate_prob[:, None] * out_flat.astype(jnp.float32)).astype(jnp.bfloat16)
    prob_grad = jnp.sum(cotangent.astype(jnp.float32) * out_flat.astype(jnp.float32), axis=1)
    finals = []
    for own_piece, copy_piece in zip(own_parts, copy_parts):
        finals.append(own_piece + jax.ops.segment_sum(copy_piece.astype(jnp.float32), copy_expert, num_segments=EXPERTS))
    return layer_out, grad_flat, prob_grad, finals[0], finals[1], finals[2]
```

```python
import jax
import jax.numpy as jnp
from jax import lax
from jax.sharding import PartitionSpec as P

ACROSS = (((1,), (1,)), ((), ()))
CONTRACT = (((0,), (0,)), ((), ()))
SPLIT_RETURN = False


def dot_f32(left, right, dims=(((1,), (0,)), ((), ()))):
    return lax.dot_general(left, right, dims, preferred_element_type=jnp.float32)


def gather_rows(block):
    return lax.all_gather(block, ("expert", "sub"), axis=0, tiled=True)


def return_rows(part):
    if not SPLIT_RETURN:
        return lax.psum_scatter(part, ("expert", "sub"), scatter_dimension=0, tiled=True)
    experts = lax.axis_size("expert")
    halves = lax.axis_size("sub")
    part = part.reshape(experts, halves, -1, part.shape[-1])
    part = lax.psum_scatter(part, "sub", scatter_dimension=1, tiled=True)
    part = lax.psum_scatter(part, "expert", scatter_dimension=0, tiled=True)
    return part.reshape(-1, part.shape[-1])


def sum_over_dp(part, axis):
    count = lax.axis_size("dp")
    if count != 2:
        return lax.psum_scatter(
            part.astype(jnp.bfloat16), "dp", scatter_dimension=axis, tiled=True
        ).astype(jnp.float32)
    mine = lax.axis_index("dp")
    width = part.shape[axis] // 2
    kept = lax.dynamic_slice_in_dim(part, mine * width, width, axis)
    given = lax.dynamic_slice_in_dim(part, (1 - mine) * width, width, axis)
    came = lax.ppermute(given.astype(jnp.bfloat16), "dp", [(0, 1), (1, 0)])
    return kept.astype(jnp.bfloat16).astype(jnp.float32) + came.astype(jnp.float32)


def on_device(
    tokens,
    cotangent,
    gate_prob,
    target_device,
    use_copy,
    hot_experts,
    copy_slot,
    gate_weight,
    up_weight,
    down_weight,
):
    gate_weight, up_weight, down_weight = gate_weight[0], up_weight[0], down_weight[0]
    copied_expert = hot_experts[copy_slot]
    expert_id = jnp.where(use_copy == 1, copied_expert[target_device], target_device)
    all_ids = gather_rows(expert_id)
    rows = gather_rows(tokens)
    scaled = (gate_prob[:, None] * cotangent.astype(jnp.float32)).astype(jnp.bfloat16)
    scaled_rows = gather_rows(scaled)
    here = (all_ids == lax.axis_index("expert"))[:, None]
    gate_in = dot_f32(rows, gate_weight)
    up_in = dot_f32(rows, up_weight)
    sigmoid_gate = jax.nn.sigmoid(gate_in)
    active = gate_in * sigmoid_gate
    hidden = jnp.where(here, active * up_in, 0.0).astype(jnp.bfloat16)
    expert_out = return_rows(dot_f32(hidden, down_weight).astype(jnp.bfloat16))
    hidden_grad = jnp.where(here, dot_f32(scaled_rows, down_weight, ACROSS), 0.0)
    gate_grad = (
        hidden_grad * up_in * sigmoid_gate * (1.0 + gate_in * (1.0 - sigmoid_gate))
    ).astype(jnp.bfloat16)
    up_grad = (hidden_grad * active).astype(jnp.bfloat16)
    row_grad = dot_f32(gate_grad, gate_weight, ACROSS) + dot_f32(up_grad, up_weight, ACROSS)
    token_grad = return_rows(row_grad.astype(jnp.bfloat16))
    down_sum = sum_over_dp(dot_f32(hidden, scaled_rows, CONTRACT), 1)
    gate_sum = sum_over_dp(dot_f32(rows, gate_grad, CONTRACT), 0)
    up_sum = sum_over_dp(dot_f32(rows, up_grad, CONTRACT), 0)
    out_wide = expert_out.astype(jnp.float32)
    layer_out = (gate_prob[:, None] * out_wide).astype(jnp.bfloat16)
    prob_grad = jnp.sum(cotangent.astype(jnp.float32) * out_wide, axis=1)
    return (layer_out, token_grad, prob_grad, gate_sum[None], up_sum[None], down_sum[None])


def solution(mesh):
    rows = ("groups", "expert", "dp", "sub")
    return jax.shard_map(
        on_device,
        mesh=mesh,
        in_specs=(
            P(rows, None),
            P(rows, None),
            P(rows),
            P(rows),
            P(rows),
            P("groups"),
            P("groups"),
            P("expert", None, "sub"),
            P("expert", None, "sub"),
            P("expert", "sub", None),
        ),
        out_specs=(
            P(rows, None),
            P(rows, None),
            P(rows),
            P(("groups", "expert"), "dp", "sub"),
            P(("groups", "expert"), "dp", "sub"),
            P(("groups", "expert"), "sub", "dp"),
        ),
        check_vma=False,
    )
```

```python
import functools

import jax
import jax.numpy as jnp
from jax import lax
from jax.experimental import pallas as pl
from jax.experimental.pallas import tpu as pltpu
from jax.sharding import PartitionSpec as P

ACROSS = (((1,), (1,)), ((), ()))
CONTRACT = (((0,), (0,)), ((), ()))
SPLIT_RETURN = False


def dot_f32(left, right, dims=(((1,), (0,)), ((), ()))):
    return lax.dot_general(left, right, dims, preferred_element_type=jnp.float32)


MESH = pl.DeviceIdType.MESH
LANES = 128
TILE = 512


def fused_kernel(
    n,
    tok_own,
    sca_own,
    gate_w,
    up_w,
    down_w,
    rows_out,
    kept_gate,
    kept_up,
    kept_down,
    came_gate,
    came_up,
    came_down,
    tok,
    sca,
    part,
    sib_in,
    z_in,
    hidden_s,
    gate_s,
    up_s,
    given_gate,
    given_up,
    given_down,
    z_send,
    z_recv,
    sib_send,
    sib_recv,
    part_send,
    part_recv,
    ret_send,
    ret_recv,
    dp_send,
    dp_recv,
):
    me = lax.axis_index("expert")
    sub = lax.axis_index("sub")
    dp = lax.axis_index("dp")
    other = 1 - sub
    last = n - 1
    count = tok_own.shape[0]
    width = sca_own.shape[1]
    half = width // 2
    both = 2 * count
    has_left = me > 0
    has_right = me < last

    def remote(src, dst, send, recv, where):
        return pltpu.make_async_remote_copy(
            src_ref=src,
            dst_ref=dst,
            send_sem=send,
            recv_sem=recv,
            device_id=where,
            device_id_type=MESH,
        )

    held = (tok, sca)

    def toward(side):
        return {"expert": me + 1 - 2 * side}

    def z_copy(kind, side, step, block):
        ref = held[kind].at[block, sub]
        return remote(
            ref, ref, z_send.at[kind, side, step], z_recv.at[kind, side, step], toward(side)
        )

    def sib_copy(kind, block, row):
        ref = held[kind].at[block, row]
        return remote(
            ref, ref, sib_send.at[kind, block], sib_recv.at[kind, block], {"sub": other}
        )

    def part_copy(block, kind):
        return remote(
            part.at[block, kind, other],
            sib_in.at[block, kind],
            part_send.at[block, kind],
            part_recv.at[block, kind],
            {"sub": other},
        )

    def ret_copy(side, dest, slot, kind):
        return remote(
            part.at[dest, kind, sub],
            z_in.at[slot, kind],
            ret_send.at[dest, kind],
            ret_recv.at[slot, kind],
            toward(side),
        )

    barrier = pltpu.get_barrier_semaphore()

    @pl.when(has_left)
    def _():
        pl.semaphore_signal(barrier, inc=1, device_id={"expert": me - 1}, device_id_type=MESH)

    @pl.when(has_right)
    def _():
        pl.semaphore_signal(barrier, inc=1, device_id={"expert": me + 1}, device_id_type=MESH)

    pl.semaphore_signal(barrier, inc=1, device_id={"sub": other}, device_id_type=MESH)
    pl.semaphore_signal(barrier, inc=1, device_id={"dp": 1 - dp}, device_id_type=MESH)
    tok[me, sub] = tok_own[...]
    sca[me, sub] = sca_own[...]
    pl.semaphore_wait(barrier, 2 + has_left.astype(jnp.int32) + has_right.astype(jnp.int32))

    for kind in range(2):

        @pl.when(has_right)
        def _():
            z_copy(kind, 0, 0, me).start()

        @pl.when(has_left)
        def _():
            z_copy(kind, 1, 0, me).start()

        sib_copy(kind, me, sub).start()

    def arrivals(step):
        for kind in range(2):
            for side in range(2):
                block = me - 1 - step if side == 0 else me + 1 + step
                valid = block >= 0 if side == 0 else block <= last
                onward = has_right if side == 0 else has_left

                @pl.when(valid)
                def _():
                    z_copy(kind, side, step, block).wait_recv()
                    sib_copy(kind, block, sub).start()

                    @pl.when(onward)
                    def _():
                        z_copy(kind, side, step + 1, block).start()

    def compute(block):
        sib_copy(0, block, other).wait_recv()
        x = tok[block, :, :, :width].reshape(both, width)
        here = tok[block, :, :, width:].reshape(both, LANES).astype(jnp.float32)
        here = here[:, :1] == me.astype(jnp.float32)
        gate_in = dot_f32(x, gate_w[...])
        up_in = dot_f32(x, up_w[...])
        sigmoid_gate = 1.0 / (1.0 + jnp.exp(-gate_in))
        active = gate_in * sigmoid_gate
        hidden = jnp.where(here, active * up_in, 0.0).astype(jnp.bfloat16)
        slope = up_in * sigmoid_gate * (1.0 + gate_in * (1.0 - sigmoid_gate))
        place = pl.ds(pl.multiple_of(block * both, both), both)
        hidden_s[place, :] = hidden

        @pl.loop(0, width // TILE)
        def _(tile):
            cols = pl.ds(pl.multiple_of(tile * TILE, TILE), TILE)
            piece = dot_f32(hidden_s[place, :], down_w[:, cols]).astype(jnp.bfloat16)
            part[block, 0, :, :, cols] = piece.reshape(2, count, TILE)

        part_copy(block, 0).start()
        sib_copy(1, block, other).wait_recv()
        s = sca[block].reshape(both, width)
        hidden_grad = jnp.where(here, dot_f32(s, down_w[...], ACROSS), 0.0)
        gate_s[place, :] = (hidden_grad * slope).astype(jnp.bfloat16)
        up_s[place, :] = (hidden_grad * active).astype(jnp.bfloat16)

        @pl.loop(0, width // TILE)
        def _(tile):
            rows = pl.ds(pl.multiple_of(tile * TILE, TILE), TILE)
            piece = dot_f32(gate_s[place, :], gate_w[rows, :], ACROSS)
            piece = piece + dot_f32(up_s[place, :], up_w[rows, :], ACROSS)
            part[block, 1, :, :, rows] = piece.astype(jnp.bfloat16).reshape(2, count, TILE)

        part_copy(block, 1).start()

    def add_sibling(dest, kind):
        part_copy(dest, kind).wait_recv()
        mine = part[dest, kind, sub].astype(jnp.float32)
        return mine + sib_in[dest, kind].astype(jnp.float32)

    def sends(turn):
        right = turn + 1 - me
        left = last - (turn + 1 - (last - me))
        return (
            (0, right, (right > me) & (right <= last), has_left, right),
            (1, left, (left < me) & (left >= 0), has_right, jnp.where(left == me - 1, n, left)),
        )

    def give_back(turn):
        for kind in range(2):
            for side, dest, valid, add, slot in sends(turn):

                @pl.when(valid)
                def _():
                    part[dest, kind, sub] = add_sibling(dest, kind).astype(jnp.bfloat16)

                    @pl.when(add)
                    def _():
                        ret_copy(side, dest, dest, kind).wait_recv()
                        part[dest, kind, sub] = (
                            part[dest, kind, sub].astype(jnp.float32)
                            + z_in[dest, kind].astype(jnp.float32)
                        ).astype(jnp.bfloat16)

                    ret_copy(side, dest, slot, kind).start()

    @pl.loop(0, n)
    def _(time):
        step = time - 1

        @pl.when(time > 0)
        def _():
            arrivals(step)

        @pl.loop(0, 2)
        def _(side):
            block = jnp.where(side == 0, me - time, me + time)
            valid = (block >= 0) & (block <= last) & ((time > 0) | (side == 0))

            @pl.when(valid)
            def _():
                compute(block)

        @pl.when(time > 0)
        def _():
            give_back(step)

    given = (given_gate, given_up, given_down)
    kept = (kept_gate, kept_up, kept_down)
    came = (came_gate, came_up, came_down)

    def dp_copy(kind):
        return remote(
            given[kind], came[kind], dp_send.at[kind], dp_recv.at[kind], {"dp": 1 - dp}
        )

    total = n * both

    def weight_grad(kind, first, into):
        if kind < 2:
            right_ref = (gate_s, up_s)[kind]

            @pl.loop(0, half // TILE)
            def _(tile):
                cols = pl.ds(pl.multiple_of(first + tile * TILE, TILE), TILE)
                rows = pl.ds(pl.multiple_of(tile * TILE, TILE), TILE)
                x = tok[:, :, :, cols].reshape(total, TILE)
                into[rows, :] = dot_f32(x, right_ref[...], CONTRACT).astype(jnp.bfloat16)

        else:

            @pl.loop(0, half // TILE)
            def _(tile):
                cols = pl.ds(pl.multiple_of(first + tile * TILE, TILE), TILE)
                there = pl.ds(pl.multiple_of(tile * TILE, TILE), TILE)
                s = sca[:, :, :, cols].reshape(total, TILE)
                into[:, there] = dot_f32(hidden_s[...], s, CONTRACT).astype(jnp.bfloat16)

    for kind in range(3):
        weight_grad(kind, (1 - dp) * half, given[kind])
        dp_copy(kind).start()

    @pl.loop(n - 1, 2 * n - 3)
    def _(turn):
        give_back(turn)

    for kind in range(3):
        weight_grad(kind, dp * half, kept[kind])

    for kind in range(2):
        rows_out[kind] = add_sibling(me, kind).astype(jnp.bfloat16)
        for slot, valid in ((me, has_left), (n, has_right)):

            @pl.when(valid)
            def _():
                ret_copy(0, me, slot, kind).wait_recv()
                rows_out[kind] = (
                    rows_out[kind].astype(jnp.float32) + z_in[slot, kind].astype(jnp.float32)
                ).astype(jnp.bfloat16)

    @pl.loop(0, n)
    def _(block):
        for kind in range(2):
            sib_copy(kind, block, sub).wait_send()
            part_copy(block, kind).wait_send()

            @pl.when(block != me)
            def _():
                ret_copy(0, block, block, kind).wait_send()

    @pl.loop(0, n - 1)
    def _(step):
        for kind in range(2):

            @pl.when(has_right & (me - step >= 0))
            def _():
                z_copy(kind, 0, step, me).wait_send()

            @pl.when(has_left & (me + step <= last))
            def _():
                z_copy(kind, 1, step, me).wait_send()

    for kind in range(3):
        dp_copy(kind).wait()


def fused(tok_own, sca_own, gate_weight, up_weight, down_weight):
    n = lax.axis_size("expert")
    count, width = sca_own.shape
    hidden_width = gate_weight.shape[1]
    half = width // 2
    b16 = jnp.bfloat16
    vmem = pl.BlockSpec(memory_space=pltpu.VMEM)
    hbm = pl.BlockSpec(memory_space=pl.ANY)
    tall = jax.ShapeDtypeStruct((half, hidden_width), b16)
    wide = jax.ShapeDtypeStruct((hidden_width, half), b16)
    dma = pltpu.SemaphoreType.DMA
    flops = 2 * 9 * n * 2 * count * width * hidden_width
    return pl.pallas_call(
        functools.partial(fused_kernel, n),
        out_shape=(
            jax.ShapeDtypeStruct((2, count, width), b16), tall, tall, wide, tall, tall, wide,
        ),
        in_specs=[vmem] * 5,
        out_specs=(vmem, vmem, vmem, vmem, hbm, hbm, hbm),
        scratch_shapes=[
            pltpu.VMEM((n, 2, count, width + LANES), b16),
            pltpu.VMEM((n, 2, count, width), b16),
            pltpu.VMEM((n, 2, 2, count, width), b16),
            pltpu.VMEM((n, 2, count, width), b16),
            pltpu.VMEM((n + 1, 2, count, width), b16),
            pltpu.VMEM((n * 2 * count, hidden_width), b16),
            pltpu.VMEM((n * 2 * count, hidden_width), b16),
            pltpu.VMEM((n * 2 * count, hidden_width), b16),
            pltpu.VMEM((half, hidden_width), b16),
            pltpu.VMEM((half, hidden_width), b16),
            pltpu.VMEM((hidden_width, half), b16),
            dma((2, 2, n)),
            dma((2, 2, n)),
            dma((2, n)),
            dma((2, n)),
            dma((n, 2)),
            dma((n, 2)),
            dma((n, 2)),
            dma((n + 1, 2)),
            dma((3,)),
            dma((3,)),
        ],
        compiler_params=pltpu.CompilerParams(
            collective_id=0, has_side_effects=True, vmem_limit_bytes=60 * 2**20
        ),
        cost_estimate=pl.CostEstimate(flops=flops, bytes_accessed=2**24, transcendentals=0),
    )(tok_own, sca_own, gate_weight, up_weight, down_weight)


def gather_rows(block):
    return lax.all_gather(block, ("expert", "sub"), axis=0, tiled=True)


def return_rows(part):
    if not SPLIT_RETURN:
        return lax.psum_scatter(part, ("expert", "sub"), scatter_dimension=0, tiled=True)
    experts = lax.axis_size("expert")
    halves = lax.axis_size("sub")
    part = part.reshape(experts, halves, -1, part.shape[-1])
    part = lax.psum_scatter(part, "sub", scatter_dimension=1, tiled=True)
    part = lax.psum_scatter(part, "expert", scatter_dimension=0, tiled=True)
    return part.reshape(-1, part.shape[-1])


def sum_over_dp(part, axis):
    count = lax.axis_size("dp")
    if count != 2:
        return lax.psum_scatter(
            part.astype(jnp.bfloat16), "dp", scatter_dimension=axis, tiled=True
        ).astype(jnp.float32)
    mine = lax.axis_index("dp")
    width = part.shape[axis] // 2
    kept = lax.dynamic_slice_in_dim(part, mine * width, width, axis)
    given = lax.dynamic_slice_in_dim(part, (1 - mine) * width, width, axis)
    came = lax.ppermute(given.astype(jnp.bfloat16), "dp", [(0, 1), (1, 0)])
    return kept.astype(jnp.bfloat16).astype(jnp.float32) + came.astype(jnp.float32)


def gathered(tokens, scaled, expert_id, gate_weight, up_weight, down_weight):
    all_ids = gather_rows(expert_id)
    rows = gather_rows(tokens)
    scaled_rows = gather_rows(scaled)
    here = (all_ids == lax.axis_index("expert"))[:, None]
    gate_in = dot_f32(rows, gate_weight)
    up_in = dot_f32(rows, up_weight)
    sigmoid_gate = jax.nn.sigmoid(gate_in)
    active = gate_in * sigmoid_gate
    hidden = jnp.where(here, active * up_in, 0.0).astype(jnp.bfloat16)
    expert_out = return_rows(dot_f32(hidden, down_weight).astype(jnp.bfloat16))
    hidden_grad = jnp.where(here, dot_f32(scaled_rows, down_weight, ACROSS), 0.0)
    gate_grad = (
        hidden_grad * up_in * sigmoid_gate * (1.0 + gate_in * (1.0 - sigmoid_gate))
    ).astype(jnp.bfloat16)
    up_grad = (hidden_grad * active).astype(jnp.bfloat16)
    row_grad = dot_f32(gate_grad, gate_weight, ACROSS) + dot_f32(up_grad, up_weight, ACROSS)
    token_grad = return_rows(row_grad.astype(jnp.bfloat16))
    down_sum = sum_over_dp(dot_f32(hidden, scaled_rows, CONTRACT), 1)
    gate_sum = sum_over_dp(dot_f32(rows, gate_grad, CONTRACT), 0)
    up_sum = sum_over_dp(dot_f32(rows, up_grad, CONTRACT), 0)
    return expert_out, token_grad, gate_sum, up_sum, down_sum


def on_device(
    tokens,
    cotangent,
    gate_prob,
    target_device,
    use_copy,
    hot_experts,
    copy_slot,
    gate_weight,
    up_weight,
    down_weight,
):
    gate_weight, up_weight, down_weight = gate_weight[0], up_weight[0], down_weight[0]
    copied_expert = hot_experts[copy_slot]
    expert_id = jnp.where(use_copy == 1, copied_expert[target_device], target_device)
    scaled = (gate_prob[:, None] * cotangent.astype(jnp.float32)).astype(jnp.bfloat16)
    if lax.axis_size("expert") <= 4 and lax.axis_size("dp") == 2 and lax.axis_size("sub") == 2:
        meta = jnp.broadcast_to(
            expert_id.astype(jnp.bfloat16)[:, None], (tokens.shape[0], LANES)
        )
        packed = jnp.concatenate((tokens, meta), axis=1)
        back, *grads = fused(packed, scaled, gate_weight, up_weight, down_weight)
        expert_out, token_grad = back[0], back[1]
        gate_sum, up_sum, down_sum = (
            kept.astype(jnp.float32) + came.astype(jnp.float32)
            for kept, came in zip(grads[:3], grads[3:])
        )
    else:
        expert_out, token_grad, gate_sum, up_sum, down_sum = gathered(
            tokens, scaled, expert_id, gate_weight, up_weight, down_weight
        )
    out_wide = expert_out.astype(jnp.float32)
    layer_out = (gate_prob[:, None] * out_wide).astype(jnp.bfloat16)
    prob_grad = jnp.sum(cotangent.astype(jnp.float32) * out_wide, axis=1)
    return (layer_out, token_grad, prob_grad, gate_sum[None], up_sum[None], down_sum[None])


def solution(mesh):
    rows = ("groups", "expert", "dp", "sub")
    return jax.shard_map(
        on_device,
        mesh=mesh,
        in_specs=(
            P(rows, None),
            P(rows, None),
            P(rows),
            P(rows),
            P(rows),
            P("groups"),
            P("groups"),
            P("expert", None, "sub"),
            P("expert", None, "sub"),
            P("expert", "sub", None),
        ),
        out_specs=(
            P(rows, None),
            P(rows, None),
            P(rows),
            P(("groups", "expert"), "dp", "sub"),
            P(("groups", "expert"), "dp", "sub"),
            P(("groups", "expert"), "sub", "dp"),
        ),
        check_vma=False,
    )
```

```python
import functools

import jax
import jax.numpy as jnp
from jax import lax
from jax.experimental import pallas as pl
from jax.experimental.pallas import tpu as pltpu
from jax.sharding import PartitionSpec as P

ACROSS = (((1,), (1,)), ((), ()))
CONTRACT = (((0,), (0,)), ((), ()))
SPLIT_RETURN = False


def dot_f32(left, right, dims=(((1,), (0,)), ((), ()))):
    return lax.dot_general(left, right, dims, preferred_element_type=jnp.float32)


MESH = pl.DeviceIdType.MESH
LANES = 128
TILE = 512


def fused_kernel(
    n,
    tok_own,
    sca_own,
    gate_any,
    up_any,
    down_any,
    rows_out,
    kept_gate,
    kept_up,
    kept_down,
    came_gate,
    came_up,
    came_down,
    tok,
    sca,
    part,
    sib_in,
    z_in,
    hidden_s,
    gate_s,
    up_s,
    given_gate,
    given_up,
    given_down,
    z_send,
    z_recv,
    sib_send,
    sib_recv,
    part_send,
    part_recv,
    ret_send,
    ret_recv,
    dp_send,
    dp_recv,
    gate_w,
    up_w,
    down_w,
    load_sem,
):
    me = lax.axis_index("expert")
    sub = lax.axis_index("sub")
    dp = lax.axis_index("dp")
    other = 1 - sub
    last = n - 1
    count = tok_own.shape[0]
    width = sca_own.shape[1]
    half = width // 2
    both = 2 * count
    has_left = me > 0
    has_right = me < last

    def remote(src, dst, send, recv, where):
        return pltpu.make_async_remote_copy(
            src_ref=src,
            dst_ref=dst,
            send_sem=send,
            recv_sem=recv,
            device_id=where,
            device_id_type=MESH,
        )

    held = (tok, sca)

    def toward(side):
        return {"expert": me + 1 - 2 * side}

    def z_copy(kind, side, step, block):
        ref = held[kind].at[block, sub]
        return remote(
            ref, ref, z_send.at[kind, side, step], z_recv.at[kind, side, step], toward(side)
        )

    def sib_copy(kind, block, row):
        ref = held[kind].at[block, row]
        return remote(
            ref, ref, sib_send.at[kind, block], sib_recv.at[kind, block], {"sub": other}
        )

    def part_copy(block, kind):
        return remote(
            part.at[block, kind, other],
            sib_in.at[block, kind],
            part_send.at[block, kind],
            part_recv.at[block, kind],
            {"sub": other},
        )

    def ret_copy(side, dest, slot, kind, piece):
        rows = pl.ds(piece * (count // 2), count // 2)
        return remote(
            part.at[dest, kind, sub, rows],
            z_in.at[slot, kind, rows],
            ret_send.at[dest, kind, piece],
            ret_recv.at[slot, kind, piece],
            toward(side),
        )

    loads = [
        pltpu.make_async_copy(src, dst, load_sem.at[index])
        for index, (src, dst) in enumerate(((gate_any, gate_w), (up_any, up_w), (down_any, down_w)))
    ]
    for load in loads:
        load.start()
    barrier = pltpu.get_barrier_semaphore()

    @pl.when(has_left)
    def _():
        pl.semaphore_signal(barrier, inc=1, device_id={"expert": me - 1}, device_id_type=MESH)

    @pl.when(has_right)
    def _():
        pl.semaphore_signal(barrier, inc=1, device_id={"expert": me + 1}, device_id_type=MESH)

    pl.semaphore_signal(barrier, inc=1, device_id={"sub": other}, device_id_type=MESH)
    pl.semaphore_signal(barrier, inc=1, device_id={"dp": 1 - dp}, device_id_type=MESH)
    tok[me, sub] = tok_own[...]
    sca[me, sub] = sca_own[...]
    pl.semaphore_wait(barrier, 2 + has_left.astype(jnp.int32) + has_right.astype(jnp.int32))

    for kind in range(2):

        @pl.when(has_right)
        def _():
            z_copy(kind, 0, 0, me).start()

        @pl.when(has_left)
        def _():
            z_copy(kind, 1, 0, me).start()

        sib_copy(kind, me, sub).start()

    for load in loads:
        load.wait()

    def arrivals(step):
        for kind in range(2):
            for side in range(2):
                block = me - 1 - step if side == 0 else me + 1 + step
                valid = block >= 0 if side == 0 else block <= last
                onward = has_right if side == 0 else has_left

                @pl.when(valid)
                def _():
                    z_copy(kind, side, step, block).wait_recv()
                    sib_copy(kind, block, sub).start()

                    @pl.when(onward)
                    def _():
                        z_copy(kind, side, step + 1, block).start()

    def compute(block):
        sib_copy(0, block, other).wait_recv()
        x = tok[block, :, :, :width].reshape(both, width)
        here = tok[block, :, :, width:].reshape(both, LANES).astype(jnp.float32)
        here = here[:, :1] == me.astype(jnp.float32)
        gate_in = dot_f32(x, gate_w[...])
        up_in = dot_f32(x, up_w[...])
        sigmoid_gate = 1.0 / (1.0 + jnp.exp(-gate_in))
        active = gate_in * sigmoid_gate
        hidden = jnp.where(here, active * up_in, 0.0).astype(jnp.bfloat16)
        slope = up_in * sigmoid_gate * (1.0 + gate_in * (1.0 - sigmoid_gate))
        place = pl.ds(pl.multiple_of(block * both, both), both)
        hidden_s[place, :] = hidden

        @pl.loop(0, width // TILE)
        def _(tile):
            cols = pl.ds(pl.multiple_of(tile * TILE, TILE), TILE)
            piece = dot_f32(hidden_s[place, :], down_w[:, cols]).astype(jnp.bfloat16)
            part[block, 0, :, :, cols] = piece.reshape(2, count, TILE)

        part_copy(block, 0).start()
        sib_copy(1, block, other).wait_recv()
        s = sca[block].reshape(both, width)
        hidden_grad = jnp.where(here, dot_f32(s, down_w[...], ACROSS), 0.0)
        gate_s[place, :] = (hidden_grad * slope).astype(jnp.bfloat16)
        up_s[place, :] = (hidden_grad * active).astype(jnp.bfloat16)

        @pl.loop(0, width // TILE)
        def _(tile):
            rows = pl.ds(pl.multiple_of(tile * TILE, TILE), TILE)
            piece = dot_f32(gate_s[place, :], gate_w[rows, :], ACROSS)
            piece = piece + dot_f32(up_s[place, :], up_w[rows, :], ACROSS)
            part[block, 1, :, :, rows] = piece.astype(jnp.bfloat16).reshape(2, count, TILE)

        part_copy(block, 1).start()

    def add_sibling(dest, kind):
        part_copy(dest, kind).wait_recv()
        mine = part[dest, kind, sub].astype(jnp.float32)
        return mine + sib_in[dest, kind].astype(jnp.float32)

    def sends(turn):
        right = turn + 1 - me
        left = last - (turn + 1 - (last - me))
        return (
            (0, right, (right > me) & (right <= last), has_left, right),
            (1, left, (left < me) & (left >= 0), has_right, jnp.where(left == me - 1, n, left)),
        )

    def give_back(turn):
        for kind in range(2):
            for side, dest, valid, add, slot in sends(turn):

                @pl.when(valid)
                def _():
                    part[dest, kind, sub] = add_sibling(dest, kind).astype(jnp.bfloat16)
                    for piece in range(2):
                        rows = pl.ds(piece * (count // 2), count // 2)

                        @pl.when(add)
                        def _():
                            ret_copy(side, dest, dest, kind, piece).wait_recv()
                            part[dest, kind, sub, rows] = (
                                part[dest, kind, sub, rows].astype(jnp.float32)
                                + z_in[dest, kind, rows].astype(jnp.float32)
                            ).astype(jnp.bfloat16)

                        ret_copy(side, dest, slot, kind, piece).start()

    @pl.loop(0, n)
    def _(time):
        step = time - 1

        @pl.when(time > 0)
        def _():
            arrivals(step)

        @pl.loop(0, 2)
        def _(side):
            block = jnp.where(side == 0, me - time, me + time)
            valid = (block >= 0) & (block <= last) & ((time > 0) | (side == 0))

            @pl.when(valid)
            def _():
                compute(block)

        @pl.when((time > 0) & (time < last))
        def _():
            give_back(step)

    given = (given_gate, given_up, given_down)
    kept = (kept_gate, kept_up, kept_down)
    came = (came_gate, came_up, came_down)

    def dp_copy(kind):
        return remote(
            given[kind], came[kind], dp_send.at[kind], dp_recv.at[kind], {"dp": 1 - dp}
        )

    total = n * both

    def weight_grad(kind, first, into):
        if kind < 2:
            right_ref = (gate_s, up_s)[kind]

            @pl.loop(0, half // TILE)
            def _(tile):
                cols = pl.ds(pl.multiple_of(first + tile * TILE, TILE), TILE)
                rows = pl.ds(pl.multiple_of(tile * TILE, TILE), TILE)
                x = tok[:, :, :, cols].reshape(total, TILE)
                into[rows, :] = dot_f32(x, right_ref[...], CONTRACT).astype(jnp.bfloat16)

        else:

            @pl.loop(0, half // TILE)
            def _(tile):
                cols = pl.ds(pl.multiple_of(first + tile * TILE, TILE), TILE)
                there = pl.ds(pl.multiple_of(tile * TILE, TILE), TILE)
                s = sca[:, :, :, cols].reshape(total, TILE)
                into[:, there] = dot_f32(hidden_s[...], s, CONTRACT).astype(jnp.bfloat16)

    def give_grad(kind):
        weight_grad(kind, (1 - dp) * half, given[kind])
        dp_copy(kind).start()

    give_grad(0)

    @pl.loop(n - 2, 2 * n - 3)
    def _(turn):
        give_back(turn)

        @pl.when(turn == n - 2)
        def _():
            give_grad(1)
            give_grad(2)

    for kind in range(3):
        weight_grad(kind, dp * half, kept[kind])

    for kind in range(2):
        rows_out[kind] = add_sibling(me, kind).astype(jnp.bfloat16)
        for slot, valid in ((me, has_left), (n, has_right)):

            @pl.when(valid)
            def _():
                for piece in range(2):
                    ret_copy(0, me, slot, kind, piece).wait_recv()
                rows_out[kind] = (
                    rows_out[kind].astype(jnp.float32) + z_in[slot, kind].astype(jnp.float32)
                ).astype(jnp.bfloat16)

    @pl.loop(0, n)
    def _(block):
        for kind in range(2):
            sib_copy(kind, block, sub).wait_send()
            part_copy(block, kind).wait_send()

            @pl.when(block != me)
            def _():
                for piece in range(2):
                    ret_copy(0, block, block, kind, piece).wait_send()

    @pl.loop(0, n - 1)
    def _(step):
        for kind in range(2):

            @pl.when(has_right & (me - step >= 0))
            def _():
                z_copy(kind, 0, step, me).wait_send()

            @pl.when(has_left & (me + step <= last))
            def _():
                z_copy(kind, 1, step, me).wait_send()

    for kind in range(3):
        dp_copy(kind).wait()


def fused(tok_own, sca_own, gate_weight, up_weight, down_weight):
    n = lax.axis_size("expert")
    count, width = sca_own.shape
    hidden_width = gate_weight.shape[1]
    half = width // 2
    b16 = jnp.bfloat16
    vmem = pl.BlockSpec(memory_space=pltpu.VMEM)
    hbm = pl.BlockSpec(memory_space=pl.ANY)
    tall = jax.ShapeDtypeStruct((half, hidden_width), b16)
    wide = jax.ShapeDtypeStruct((hidden_width, half), b16)
    dma = pltpu.SemaphoreType.DMA
    flops = 2 * 9 * n * 2 * count * width * hidden_width
    return pl.pallas_call(
        functools.partial(fused_kernel, n),
        out_shape=(
            jax.ShapeDtypeStruct((2, count, width), b16), tall, tall, wide, tall, tall, wide,
        ),
        in_specs=[vmem, vmem, hbm, hbm, hbm],
        out_specs=(vmem, vmem, vmem, vmem, hbm, hbm, hbm),
        scratch_shapes=[
            pltpu.VMEM((n, 2, count, width + LANES), b16),
            pltpu.VMEM((n, 2, count, width), b16),
            pltpu.VMEM((n, 2, 2, count, width), b16),
            pltpu.VMEM((n, 2, count, width), b16),
            pltpu.VMEM((n + 1, 2, count, width), b16),
            pltpu.VMEM((n * 2 * count, hidden_width), b16),
            pltpu.VMEM((n * 2 * count, hidden_width), b16),
            pltpu.VMEM((n * 2 * count, hidden_width), b16),
            pltpu.VMEM((half, hidden_width), b16),
            pltpu.VMEM((half, hidden_width), b16),
            pltpu.VMEM((hidden_width, half), b16),
            dma((2, 2, n)),
            dma((2, 2, n)),
            dma((2, n)),
            dma((2, n)),
            dma((n, 2)),
            dma((n, 2)),
            dma((n, 2, 2)),
            dma((n + 1, 2, 2)),
            dma((3,)),
            dma((3,)),
            pltpu.VMEM(gate_weight.shape, b16),
            pltpu.VMEM(up_weight.shape, b16),
            pltpu.VMEM(down_weight.shape, b16),
            dma((3,)),
        ],
        compiler_params=pltpu.CompilerParams(
            collective_id=0, has_side_effects=True, vmem_limit_bytes=60 * 2**20
        ),
        cost_estimate=pl.CostEstimate(flops=flops, bytes_accessed=2**24, transcendentals=0),
    )(tok_own, sca_own, gate_weight, up_weight, down_weight)


def gather_rows(block):
    return lax.all_gather(block, ("expert", "sub"), axis=0, tiled=True)


def return_rows(part):
    if not SPLIT_RETURN:
        return lax.psum_scatter(part, ("expert", "sub"), scatter_dimension=0, tiled=True)
    experts = lax.axis_size("expert")
    halves = lax.axis_size("sub")
    part = part.reshape(experts, halves, -1, part.shape[-1])
    part = lax.psum_scatter(part, "sub", scatter_dimension=1, tiled=True)
    part = lax.psum_scatter(part, "expert", scatter_dimension=0, tiled=True)
    return part.reshape(-1, part.shape[-1])


def sum_over_dp(part, axis):
    count = lax.axis_size("dp")
    if count != 2:
        return lax.psum_scatter(
            part.astype(jnp.bfloat16), "dp", scatter_dimension=axis, tiled=True
        ).astype(jnp.float32)
    mine = lax.axis_index("dp")
    width = part.shape[axis] // 2
    kept = lax.dynamic_slice_in_dim(part, mine * width, width, axis)
    given = lax.dynamic_slice_in_dim(part, (1 - mine) * width, width, axis)
    came = lax.ppermute(given.astype(jnp.bfloat16), "dp", [(0, 1), (1, 0)])
    return kept.astype(jnp.bfloat16).astype(jnp.float32) + came.astype(jnp.float32)


def gathered(tokens, scaled, expert_id, gate_weight, up_weight, down_weight):
    all_ids = gather_rows(expert_id)
    rows = gather_rows(tokens)
    scaled_rows = gather_rows(scaled)
    here = (all_ids == lax.axis_index("expert"))[:, None]
    gate_in = dot_f32(rows, gate_weight)
    up_in = dot_f32(rows, up_weight)
    sigmoid_gate = jax.nn.sigmoid(gate_in)
    active = gate_in * sigmoid_gate
    hidden = jnp.where(here, active * up_in, 0.0).astype(jnp.bfloat16)
    expert_out = return_rows(dot_f32(hidden, down_weight).astype(jnp.bfloat16))
    hidden_grad = jnp.where(here, dot_f32(scaled_rows, down_weight, ACROSS), 0.0)
    gate_grad = (
        hidden_grad * up_in * sigmoid_gate * (1.0 + gate_in * (1.0 - sigmoid_gate))
    ).astype(jnp.bfloat16)
    up_grad = (hidden_grad * active).astype(jnp.bfloat16)
    row_grad = dot_f32(gate_grad, gate_weight, ACROSS) + dot_f32(up_grad, up_weight, ACROSS)
    token_grad = return_rows(row_grad.astype(jnp.bfloat16))
    down_sum = sum_over_dp(dot_f32(hidden, scaled_rows, CONTRACT), 1)
    gate_sum = sum_over_dp(dot_f32(rows, gate_grad, CONTRACT), 0)
    up_sum = sum_over_dp(dot_f32(rows, up_grad, CONTRACT), 0)
    return expert_out, token_grad, gate_sum, up_sum, down_sum


def on_device(
    tokens,
    cotangent,
    gate_prob,
    target_device,
    use_copy,
    hot_experts,
    copy_slot,
    gate_weight,
    up_weight,
    down_weight,
):
    gate_weight, up_weight, down_weight = gate_weight[0], up_weight[0], down_weight[0]
    slots = jnp.arange(hot_experts.shape[0], dtype=jnp.int32)
    targets = jnp.arange(copy_slot.shape[0], dtype=jnp.int32)
    copied_expert = jnp.sum(
        jnp.where(copy_slot[:, None] == slots[None, :], hot_experts[None, :], 0), axis=1
    )
    copied = jnp.sum(
        jnp.where(target_device[:, None] == targets[None, :], copied_expert[None, :], 0), axis=1
    )
    expert_id = jnp.where(use_copy == 1, copied, target_device)
    scaled = (gate_prob[:, None] * cotangent.astype(jnp.float32)).astype(jnp.bfloat16)
    if lax.axis_size("expert") <= 4 and lax.axis_size("dp") == 2 and lax.axis_size("sub") == 2:
        meta = jnp.broadcast_to(
            expert_id.astype(jnp.bfloat16)[:, None], (tokens.shape[0], LANES)
        )
        packed = jnp.concatenate((tokens, meta), axis=1)
        back, *grads = fused(packed, scaled, gate_weight, up_weight, down_weight)
        expert_out, token_grad = back[0], back[1]
        gate_sum, up_sum, down_sum = (
            kept.astype(jnp.float32) + came.astype(jnp.float32)
            for kept, came in zip(grads[:3], grads[3:])
        )
    else:
        expert_out, token_grad, gate_sum, up_sum, down_sum = gathered(
            tokens, scaled, expert_id, gate_weight, up_weight, down_weight
        )
    out_wide = expert_out.astype(jnp.float32)
    layer_out = (gate_prob[:, None] * out_wide).astype(jnp.bfloat16)
    prob_grad = jnp.sum(cotangent.astype(jnp.float32) * out_wide, axis=1)
    return (layer_out, token_grad, prob_grad, gate_sum[None], up_sum[None], down_sum[None])


def solution(mesh):
    rows = ("groups", "expert", "dp", "sub")
    return jax.shard_map(
        on_device,
        mesh=mesh,
        in_specs=(
            P(rows, None),
            P(rows, None),
            P(rows),
            P(rows),
            P(rows),
            P("groups"),
            P("groups"),
            P("expert", None, "sub"),
            P("expert", None, "sub"),
            P("expert", "sub", None),
        ),
        out_specs=(
            P(rows, None),
            P(rows, None),
            P(rows),
            P(("groups", "expert"), "dp", "sub"),
            P(("groups", "expert"), "dp", "sub"),
            P(("groups", "expert"), "sub", "dp"),
        ),
        check_vma=False,
    )
```
